32 devices in a mesh: space: 8 (over y, x, core), chaos: 4 (over z).
Axes of the slice: x: 2, y: 2, z: 4, core: 2. Of those that a mesh axis runs over, the one named last changes fastest.
Arguments:
- field: bfloat16 [168, 131072], P('chaos', 'space'), may hold values from -6 to 6
- stiffness: bfloat16 [2048, 4096], P(('space', 'chaos')), may hold values from -0.75 to 0.75
- kl_coef: float32 [9, 2048], P(None, ('space', 'chaos')), may hold values from -3 to 3
- triple_mode: int32 [2688], replicated, may hold values from 0 to 7
- triple_row: int32 [2688], replicated, may hold values from 0 to 167
- triple_col: int32 [2688], replicated, may hold values from 0 to 167
- triple_value: float32 [2688], replicated, may hold values from -3 to 3
- die_elem: int32 [4096], P(('space', 'chaos')), may hold values from 0 to 63
- die_side: int32 [4096], P(('space', 'chaos')), may hold values from 0 to 5
- seg_owner: int32 [4096], P(('space', 'chaos')), may hold values from 0 to 31, as said below
- seg_face: int32 [4096], P(('space', 'chaos')), may hold values from 0 to 63
- die_mortar: bfloat16 [4096, 256], P(('space', 'chaos')), may hold values from -1.5 to 1.5
- int_mortar: bfloat16 [4096, 256], P(('space', 'chaos')), may hold values from -1.5 to 1.5
- bump_coef: bfloat16 [4096, 9], P(('space', 'chaos')), may hold values from -3 to 3
- int_elem: int32 [2048], P(('space', 'chaos')), may hold values from 0 to 63
- int_side: int32 [2048], P(('space', 'chaos')), may hold values from 0 to 5
Outputs:
- response: bfloat16 [168, 131072], P('chaos', 'space')
The draws below stay inside these ranges and needn't reach their ends.
Inputs may be any that keep to these rules, and one draw needn't show every extreme that they name: `seg_owner`: in each device's block of 128 segments no owner appears more than 8 times; one owner device receives exactly 8 segments from every device's block.
All inputs are finite; a program needn't handle non-finite values.
Results may differ from the reference program's by a relative error of at most 0.006.
Values may be sent and summed in bfloat16 or wider, within the bound.
A program may use at most 64 MiB of HBM per device.

```python
import jax
import jax.numpy as jnp
import numpy as np
from jax import lax

P_SIZE = 168
MODES = 8
ELEM_NODES = 64
E_DEV = 64
SEG_DEV = 128
IFACE_DEV = 64
CAP = 8
TRIPLES = 2688
NELEM = 2048
NDOF = 131072
SEGS = 4096
IFACES = 2048
DEVICES = 32


def draw_seg_owner(key, part):
    base_key = jax.random.fold_in(key, 11)
    special_key, block_keys = jax.random.split(base_key)
    special = jax.random.randint(special_key, (), 0, DEVICES).astype(jnp.int32)

    def one_block(block_key):
        first_key, second_key = jax.random.split(block_key)
        shuffled = jax.random.permutation(first_key, DEVICES * CAP)
        owners = (shuffled // CAP).astype(jnp.int32)
        ranking = jnp.argsort((owners == special).astype(jnp.int32), stable=True)
        others = owners[ranking][:SEG_DEV - CAP]
        filled = jnp.concatenate([jnp.full((CAP,), special, jnp.int32), others])
        return filled[jax.random.permutation(second_key, SEG_DEV)]
    return jax.vmap(one_block)(jax.random.split(block_keys, DEVICES)).reshape(-1).astype(jnp.int32)


def touch_ends(entries, key, smallest, largest):
    longest = entries.shape.index(max(entries.shape))
    spots = []
    for shift in (0, 1):
        where = [jax.random.randint(jax.random.fold_in(key, axis), (), 0, length) for axis, length in enumerate(entries.shape)]
        where[longest] = (where[longest] + shift) % entries.shape[longest]
        spots.append(tuple(where))
    return entries.at[spots[0]].set(smallest).at[spots[1]].set(largest)


def block_scale(own_key, dims, pieces, least, largest):
    def one(axis_at, blocks):
        steps = jax.random.uniform(jax.random.fold_in(jax.random.fold_in(own_key, 6), axis_at), (blocks,), jnp.float32, least / len(pieces), largest / len(pieces))
        return jnp.repeat(jnp.exp(steps), dims[axis_at] // blocks).reshape((-1,) + (1,) * (len(dims) - axis_at - 1))

    loudness = one(*pieces[0])
    for cut in pieces[1:]:
        loudness = loudness * one(*cut)
    return loudness


def scatter_about(key, shape, width, reach, cuts=(), held_as=jnp.bfloat16):
    values = jax.random.normal(key, shape, jnp.float32) * width
    if len(cuts) > 0:
        values = block_scale(key, shape, cuts, -0.22, 0.18) * values
    return jnp.clip(values, min=-reach, max=reach).astype(held_as)


def setup_inputs(seed: int = 0) -> dict:
    seeds = jax.random.split(jax.random.key(seed), 17)
    field = scatter_about(seeds[0], (P_SIZE, NDOF), 1.0, 6.0, ((0, 4), (1, 8)))
    stiffness = scatter_about(seeds[1], (NELEM, ELEM_NODES * ELEM_NODES), ELEM_NODES ** -0.5, 0.75, ((0, 32),))
    kl_coef = scatter_about(seeds[2], (MODES + 1, NELEM), 0.5, 3.0, ((1, 32),), jnp.float32)
    triple_mode = touch_ends(jax.random.randint(seeds[3], (TRIPLES,), 0, MODES), jax.random.fold_in(seeds[3], 1), 0, MODES - 1).astype(jnp.int32)
    triple_row = touch_ends(jax.random.randint(seeds[4], (TRIPLES,), 0, P_SIZE), jax.random.fold_in(seeds[4], 1), 0, P_SIZE - 1).astype(jnp.int32)
    triple_col = touch_ends(jax.random.randint(seeds[5], (TRIPLES,), 0, P_SIZE), jax.random.fold_in(seeds[5], 1), 0, P_SIZE - 1).astype(jnp.int32)
    triple_value = scatter_about(seeds[6], (TRIPLES,), 0.5, 3.0, (), jnp.float32)
    die_elem = touch_ends(jax.random.randint(seeds[7], (SEGS,), 0, E_DEV), jax.random.fold_in(seeds[7], 1), 0, E_DEV - 1).astype(jnp.int32)
    die_side = touch_ends(jax.random.randint(seeds[8], (SEGS,), 0, 6), jax.random.fold_in(seeds[8], 1), 0, 5).astype(jnp.int32)
    seg_owner = draw_seg_owner(jax.random.fold_in(seeds[16], 71), 0)
    seg_face = touch_ends(jax.random.randint(seeds[10], (SEGS,), 0, IFACE_DEV), jax.random.fold_in(seeds[10], 1), 0, IFACE_DEV - 1).astype(jnp.int32)
    die_mortar = scatter_about(seeds[11], (SEGS, 256), 16 ** -0.5, 1.5, ((0, 32),))
    int_mortar = scatter_about(seeds[12], (SEGS, 256), 16 ** -0.5, 1.5, ((0, 32),))
    bump_coef = scatter_about(seeds[13], (SEGS, MODES + 1), 0.5, 3.0, ((0, 32),))
    int_elem = touch_ends(jax.random.randint(seeds[14], (IFACES,), 0, E_DEV), jax.random.fold_in(seeds[14], 1), 0, E_DEV - 1).astype(jnp.int32)
    int_side = touch_ends(jax.random.randint(seeds[15], (IFACES,), 0, 6), jax.random.fold_in(seeds[15], 1), 0, 5).astype(jnp.int32)
    return {"field": field, "stiffness": stiffness, "kl_coef": kl_coef, "triple_mode": triple_mode, "triple_row": triple_row, "triple_col": triple_col, "triple_value": triple_value, "die_elem": die_elem, "die_side": die_side, "seg_owner": seg_owner, "seg_face": seg_face, "die_mortar": die_mortar, "int_mortar": int_mortar, "bump_coef": bump_coef, "int_elem": int_elem, "int_side": int_side}


def face_nodes():
    node_rows = []
    for side_idx in range(6):
        normal_axis = side_idx // 2
        plane_level = 3 * (side_idx % 2)
        row_nodes = []
        for first_coord in range(4):
            for second_coord in range(4):
                position = [first_coord, second_coord]
                position.insert(normal_axis, plane_level)
                row_nodes.append(16 * position[0] + 4 * position[1] + position[2])
        node_rows.append(row_nodes)
    return np.array(node_rows, dtype=np.int32)


def reference(field, stiffness, kl_coef, triple_mode, triple_row, triple_col, triple_value, die_elem, die_side, seg_owner, seg_face, die_mortar, int_mortar, bump_coef, int_elem, int_side):
    coupling = jnp.zeros((MODES, P_SIZE, P_SIZE), jnp.float32).at[triple_mode, triple_row, triple_col].add(triple_value).astype(jnp.bfloat16)
    node_table = jnp.asarray(face_nodes())
    kl_nodes = jnp.repeat(kl_coef, ELEM_NODES, axis=1)
    mixed = kl_nodes[0] * field.astype(jnp.float32)
    for mode_idx in range(MODES):
        mixed = mixed + kl_nodes[mode_idx + 1] * jnp.dot(coupling[mode_idx], field, preferred_element_type=jnp.float32)
    mixed = lax.optimization_barrier(mixed.astype(jnp.bfloat16))
    blocks = stiffness.astype(jnp.float32).reshape(NELEM, ELEM_NODES, ELEM_NODES)
    local_out = jnp.einsum("eab,peb->pea", blocks, mixed.astype(jnp.float32).reshape(P_SIZE, NELEM, ELEM_NODES)).reshape(P_SIZE, NDOF)

    seg_index = jnp.arange(SEGS, dtype=jnp.int32)
    die_global = E_DEV * (seg_index // SEG_DEV) + die_elem
    die_nodes = (die_global[:, None] * ELEM_NODES + node_table[die_side]).astype(jnp.int32)
    face_global = (IFACE_DEV * seg_owner + seg_face).astype(jnp.int32)
    int_global = E_DEV * seg_owner + int_elem[face_global]
    int_nodes = (int_global[:, None] * ELEM_NODES + node_table[int_side[face_global]]).astype(jnp.int32)

    die_mats = die_mortar.astype(jnp.float32).reshape(SEGS, 16, 16)
    int_mats = int_mortar.astype(jnp.float32).reshape(SEGS, 16, 16)
    die_face = field[:, die_nodes].astype(jnp.float32)
    die_proj = lax.optimization_barrier(jnp.einsum("sgf,psf->sgp", die_mats, die_face).astype(jnp.bfloat16))
    int_face = field[:, int_nodes].astype(jnp.float32)
    int_proj = jnp.einsum("sgf,psf->sgp", int_mats, int_face)
    jump_vals = lax.optimization_barrier((die_proj.astype(jnp.float32) - int_proj).astype(jnp.bfloat16))

    weights = bump_coef.astype(jnp.float32)
    accum = weights[:, 0][:, None, None] * jump_vals.astype(jnp.float32)
    flat_jump = jump_vals.reshape(SEGS * 16, P_SIZE)
    for mode_idx in range(MODES):
        term = jnp.dot(flat_jump, coupling[mode_idx].T, preferred_element_type=jnp.float32).reshape(SEGS, 16, P_SIZE)
        accum = accum + weights[:, mode_idx + 1][:, None, None] * term
    seg_flux = lax.optimization_barrier(accum.astype(jnp.bfloat16)).astype(jnp.float32)

    die_back = jnp.einsum("sgf,sgp->psf", die_mats, seg_flux).reshape(P_SIZE, SEGS * 16)
    int_back = jnp.einsum("sgf,sgp->psf", int_mats, seg_flux).reshape(P_SIZE, SEGS * 16)
    result = local_out.at[:, die_nodes.reshape(-1)].add(die_back)
    result = result.at[:, int_nodes.reshape(-1)].add(-int_back)
    return result.astype(jnp.bfloat16)
```

```python
import functools

import jax
import jax.numpy as jnp
import numpy as np
from jax import lax
from jax.experimental import pallas as pl
from jax.experimental.pallas import tpu as pltpu
from jax.sharding import PartitionSpec as P

ELEM_NODES = 64
LANES = 128
FACE = 16
VMEM_LIMIT = 56 * 1024 * 1024
NT = (((1,), (1,)), ((), ()))
NN = (((1,), (0,)), ((), ()))


def face_nodes():
    node_rows = []
    for side_idx in range(6):
        normal_axis = side_idx // 2
        plane_level = 3 * (side_idx % 2)
        row_nodes = []
        for first_coord in range(4):
            for second_coord in range(4):
                position = [first_coord, second_coord]
                position.insert(normal_axis, plane_level)
                row_nodes.append(16 * position[0] + 4 * position[1] + position[2])
        node_rows.append(row_nodes)
    return np.array(node_rows, dtype=np.int32)


def side_nodes(side_ids):
    node_table = jnp.asarray(face_nodes())
    side_hot = (side_ids[:, None] == jnp.arange(6, dtype=jnp.int32)[None, :]).astype(jnp.int32)
    return jnp.sum(side_hot[:, :, None] * node_table[None, :, :], axis=1)


def mm(a, b, dims=NN):
    return lax.dot_general(a, b, dims, preferred_element_type=jnp.float32)


def iota(shape, dim):
    return lax.broadcasted_iota(jnp.int32, shape, dim)


def hot(mask):
    return jnp.where(mask, 1.0, 0.0).astype(jnp.bfloat16)


def perm_hot(shape, chaos_dim, wide_dim, part, padded):
    i = iota(shape, chaos_dim)
    return hot(iota(shape, wide_dim) == i // part * padded + i % part)


def block_diag(flat):
    spread = mm(hot(iota((LANES, 8), 0) // FACE == iota((LANES, 8), 1)), flat)
    own_row = iota((LANES, 256), 1) // FACE == iota((LANES, 256), 0) % FACE
    spread = jnp.where(own_row, spread, 0.0).astype(jnp.bfloat16)
    fold = hot(iota((256, LANES), 0) % FACE == iota((256, LANES), 1) % FACE)
    tiled = mm(spread, fold)
    same = iota((LANES, LANES), 0) // FACE == iota((LANES, LANES), 1) // FACE
    return jnp.where(same, tiled, 0.0).astype(jnp.bfloat16)


def node_hot(target_row):
    return hot(iota((8 * LANES, LANES), 0) == target_row)


def faces_of(fp_ref, pair_ref, target_ref, group):
    blocks = jnp.concatenate([fp_ref[pair_ref[group * 8 + j]] for j in range(8)], axis=1)
    return mm(blocks, node_hot(target_ref[group])).astype(jnp.bfloat16)


def pack_kernel(owner_col_ref, owner_row_ref, die_ref, int_ref, small_ref, die_out, meta_out, small_out, *, cap):
    segs = owner_row_ref.shape[1]
    slots = die_out.shape[0]
    same = owner_col_ref[...] == owner_row_ref[...]
    before = iota((segs, segs), 0) < iota((segs, segs), 1)
    rank = jnp.sum(jnp.where(same & before, 1.0, 0.0), axis=0, keepdims=True).astype(jnp.int32)
    place = hot(iota((slots, segs), 0) == owner_row_ref[...] * cap + rank)
    die_out[...] = mm(place, die_ref[...]).astype(jnp.bfloat16)
    small = mm(place, small_ref[...])
    small_out[...] = small
    meta_out[:, :256] = mm(place, int_ref[...]).astype(jnp.bfloat16)
    meta_out[:, 256:] = small.astype(jnp.bfloat16)


def project_kernel(pair_ref, f_ref, die_ref, target_ref, fp_out, proj_out, *, part, padded):
    chaos, wide = fp_out.shape[1], f_ref.shape[0]
    perm = perm_hot((chaos, wide), 0, 1, part, padded)
    for p in range(fp_out.shape[0]):
        fp_out[p] = mm(perm, f_ref[:, p * LANES:(p + 1) * LANES]).astype(jnp.bfloat16)

    def step(g, carry):
        face = faces_of(fp_out, pair_ref, target_ref, g)
        mats = block_diag(die_ref[pl.ds(pl.multiple_of(g * 8, 8), 8), :].astype(jnp.bfloat16))
        proj_out[g] = mm(face, mats, NT).astype(jnp.bfloat16)
        return carry

    lax.fori_loop(0, proj_out.shape[0], step, 0, unroll=2)


def mix(coupling_ref, block, weights):
    total = weights[0:1] * block.astype(jnp.float32)
    for k in range(coupling_ref.shape[0]):
        total = total + weights[k + 1:k + 2] * mm(coupling_ref[k], block)
    return total.astype(jnp.bfloat16)


def element_kernel(pair_ref, fp_ref, coupling_ref, kl_ref, stiff_ref, int_ref, target_ref, out_ref, own_out):
    def step(p, carry):
        block = jnp.concatenate([fp_ref[2 * p], fp_ref[2 * p + 1]], axis=1)
        mixed = mix(coupling_ref, block, kl_ref[p])
        out_ref[2 * p] = mm(mixed[:, :LANES], stiff_ref[2 * p], NT)
        out_ref[2 * p + 1] = mm(mixed[:, LANES:], stiff_ref[2 * p + 1], NT)
        return carry

    lax.fori_loop(0, fp_ref.shape[0] // 2, step, 0)

    def own_step(g, carry):
        face = faces_of(fp_ref, pair_ref, target_ref, g)
        mats = block_diag(int_ref[pl.ds(pl.multiple_of(g * 8, 8), 8), :].astype(jnp.bfloat16))
        own_out[g] = mm(face, mats, NT)
        return carry

    lax.fori_loop(0, own_out.shape[0], own_step, 0, unroll=2)


def flux_kernel(recv_ref, own_ref, coupling_ref, coef_ref, flux_out):
    def step(p, carry):
        jump = [
            (recv_ref[2 * p + h].astype(jnp.float32) - own_ref[2 * p + h]).astype(jnp.bfloat16)
            for h in range(2)
        ]
        flux = mix(coupling_ref, jnp.concatenate(jump, axis=1), coef_ref[p])
        flux_out[2 * p] = flux[:, :LANES]
        flux_out[2 * p + 1] = flux[:, LANES:]
        return carry

    lax.fori_loop(0, recv_ref.shape[0] // 2, step, 0)


def scatter_step(pair_ref, flux_ref, mort_ref, target_ref, acc_ref, g, sign):
    mats = block_diag(mort_ref[pl.ds(pl.multiple_of(g * 8, 8), 8), :].astype(jnp.bfloat16))
    spread = mm(mats, node_hot(target_ref[g]), NT).astype(jnp.bfloat16)
    back = mm(flux_ref[g], spread)
    for j in range(8):
        pair = pair_ref[g * 8 + j]
        acc_ref[pair] = acc_ref[pair] + sign * back[:, j * LANES:(j + 1) * LANES]


def own_back_kernel(pair_ref, flux_ref, int_ref, target_ref, start_ref, acc_out):
    acc_out[...] = start_ref[...]

    def step(g, carry):
        scatter_step(pair_ref, flux_ref, int_ref, target_ref, acc_out, g, -1.0)
        return carry

    lax.fori_loop(0, flux_ref.shape[0], step, 0, unroll=2)


def die_back_kernel(pair_ref, flux_ref, die_ref, target_ref, start_ref, out_ref, acc_ref, *, part, padded):
    acc_ref[...] = start_ref[...]

    def step(g, carry):
        scatter_step(pair_ref, flux_ref, die_ref, target_ref, acc_ref, g, 1.0)
        return carry

    lax.fori_loop(0, flux_ref.shape[0], step, 0, unroll=2)
    chaos, wide = acc_ref.shape[1], out_ref.shape[0]
    perm = perm_hot((wide, chaos), 1, 0, part, padded)
    for p in range(acc_ref.shape[0]):
        block = mm(perm, acc_ref[p].astype(jnp.bfloat16)).astype(jnp.bfloat16)
        out_ref[:, p * LANES:(p + 1) * LANES] = block


def call(kernel, outs, args, scalars=0, scratch=()):
    spaces = [pltpu.SMEM] * scalars + [pltpu.VMEM] * (len(args) - scalars)
    return pl.pallas_call(
        kernel,
        out_shape=outs,
        in_specs=[pl.BlockSpec(memory_space=s) for s in spaces],
        out_specs=jax.tree.map(lambda _: pl.BlockSpec(memory_space=pltpu.VMEM), outs),
        scratch_shapes=scratch,
        compiler_params=pltpu.CompilerParams(vmem_limit_bytes=VMEM_LIMIT),
    )(*args)


def dense_coupling(triple_mode, triple_row, triple_col, triple_value, mode_count, chaos_width):
    flat_index = triple_mode * chaos_width + triple_row
    left_hot = (
        flat_index[:, None] == jnp.arange(mode_count * chaos_width, dtype=jnp.int32)[None, :]
    ).astype(jnp.float32)
    right_hot = (triple_col[:, None] == jnp.arange(chaos_width, dtype=jnp.int32)[None, :]).astype(
        jnp.float32
    ) * triple_value[:, None]
    summed = jnp.einsum(
        "ta,tb->ab",
        left_hot,
        right_hot,
        precision=lax.Precision.HIGHEST,
        preferred_element_type=jnp.float32,
    )
    return summed.reshape(mode_count, chaos_width, chaos_width).astype(jnp.bfloat16)


def slot_targets(elem, side):
    slots = elem.shape[0]
    lane_block = (jnp.arange(slots, dtype=jnp.int32) % 8) * LANES + (elem % 2) * ELEM_NODES
    target = lane_block[:, None] + side_nodes(side)
    return elem // 2, target.reshape(slots // 8, 1, LANES)


def lane_weights(rows, repeat):
    rows = jnp.pad(rows, ((0, 16 - rows.shape[0]), (0, 0)))
    per = 256 // repeat
    tiles = rows.shape[1] // per
    rows = jnp.transpose(rows.reshape(16, tiles, per), (1, 0, 2))
    spread = (jnp.arange(per)[:, None] == jnp.arange(256)[None, :] // repeat).astype(jnp.float32)
    return jnp.einsum("tkp,pl->tkl", rows, spread, precision=lax.Precision.HIGHEST)


def local(
    field,
    stiffness,
    kl_coef,
    triple_mode,
    triple_row,
    triple_col,
    triple_value,
    die_elem,
    die_side,
    seg_owner,
    seg_face,
    die_mortar,
    int_mortar,
    bump_coef,
    int_elem,
    int_side,
):
    n_chaos = lax.axis_size("chaos")
    devices = lax.axis_size("space") * n_chaos
    part, local_nodes = field.shape
    chaos = part * n_chaos
    nodes = local_nodes // n_chaos
    padded = -(-part // 16) * 16
    segs = die_elem.shape[0]
    cap = max(2, 2 * segs // devices)
    slots = devices * cap
    groups = slots // 8
    pairs = nodes // LANES
    modes = bump_coef.shape[1] - 1
    bf16, f32 = jnp.bfloat16, jnp.float32
    axes = ("space", "chaos")

    sent = jnp.pad(field, ((0, padded - part), (0, 0))).reshape(padded, n_chaos, nodes)
    sent = jnp.transpose(sent, (1, 0, 2))
    wide = lax.all_to_all(sent, "chaos", split_axis=0, concat_axis=0, tiled=True)
    wide = wide.reshape(n_chaos * padded, nodes)

    ints = jnp.stack([seg_face, die_elem, die_side], axis=1).astype(bf16)
    small = jnp.pad(jnp.concatenate([bump_coef, ints], axis=1), ((0, 0), (0, LANES - modes - 4)))
    die_slots, meta, small_slots = call(
        functools.partial(pack_kernel, cap=cap),
        (
            jax.ShapeDtypeStruct((slots, 256), bf16),
            jax.ShapeDtypeStruct((slots, 256 + LANES), bf16),
            jax.ShapeDtypeStruct((slots, LANES), f32),
        ),
        (seg_owner[:, None], seg_owner[None, :], die_mortar, int_mortar, small),
    )
    meta = lax.all_to_all(meta, axes, split_axis=0, concat_axis=0, tiled=True)
    die_ids = small_slots[:, modes + 2:modes + 4].astype(jnp.int32)
    die_pair, die_target = slot_targets(die_ids[:, 0], die_ids[:, 1])

    coupling = dense_coupling(triple_mode, triple_row, triple_col, triple_value, modes, chaos)
    kl_lanes = lane_weights(kl_coef, ELEM_NODES)
    blocks = stiffness.reshape(pairs, 2, ELEM_NODES, 1, ELEM_NODES)
    on_diag = jnp.eye(2, dtype=bool)[None, :, None, :, None]
    stiff = jnp.where(on_diag, blocks, jnp.zeros((), bf16)).reshape(pairs, LANES, LANES)

    fp, proj = call(
        functools.partial(project_kernel, part=part, padded=padded),
        (
            jax.ShapeDtypeStruct((pairs, chaos, LANES), bf16),
            jax.ShapeDtypeStruct((groups, chaos, LANES), bf16),
        ),
        (die_pair, wide, die_slots, die_target),
        1,
    )

    def exchange(values):
        per = devices // groups
        values = values.reshape(groups, chaos, per, LANES // per)
        values = jnp.transpose(values, (0, 2, 1, 3)).reshape(devices, chaos, LANES // per)
        values = lax.all_to_all(values, axes, split_axis=0, concat_axis=0, tiled=True)
        values = values.reshape(groups, per, chaos, LANES // per)
        return jnp.transpose(values, (0, 2, 1, 3)).reshape(groups, chaos, LANES)

    recv = exchange(proj)

    int_slots = meta[:, :256]
    recv_small = meta[:, 256:256 + modes + 2].astype(f32)
    coef_lanes = lane_weights(recv_small[:, :modes + 1].T, FACE)
    face_hot = recv_small[:, modes + 1].astype(jnp.int32)[:, None] == jnp.arange(int_elem.shape[0])[None, :]
    own_elem = jnp.sum(jnp.where(face_hot, int_elem[None, :], 0), axis=1)
    own_side = jnp.sum(jnp.where(face_hot, int_side[None, :], 0), axis=1)
    own_pair, own_target = slot_targets(own_elem, own_side)

    local_out, own_proj = call(
        element_kernel,
        (
            jax.ShapeDtypeStruct((pairs, chaos, LANES), f32),
            jax.ShapeDtypeStruct((groups, chaos, LANES), f32),
        ),
        (own_pair, fp, coupling, kl_lanes, stiff, int_slots, own_target),
        1,
    )
    flux = call(
        flux_kernel,
        jax.ShapeDtypeStruct((groups, chaos, LANES), bf16),
        (recv, own_proj, coupling, coef_lanes),
    )
    back_flux = exchange(flux)
    local_out = call(
        own_back_kernel,
        jax.ShapeDtypeStruct((pairs, chaos, LANES), f32),
        (own_pair, flux, int_slots, own_target, local_out),
        1,
    )
    result = call(
        functools.partial(die_back_kernel, part=part, padded=padded),
        jax.ShapeDtypeStruct((n_chaos * padded, nodes), bf16),
        (die_pair, back_flux, die_slots, die_target, local_out),
        1,
        (pltpu.VMEM((pairs, chaos, LANES), f32),),
    )
    result = result.reshape(n_chaos, padded, nodes)
    returned = lax.all_to_all(result, "chaos", split_axis=0, concat_axis=0, tiled=True)
    return jnp.transpose(returned[:, :part], (1, 0, 2)).reshape(part, local_nodes)


def solution(mesh):
    in_specs = (
        P("chaos", "space"),
        P(("space", "chaos"), None),
        P(None, ("space", "chaos")),
        P(),
        P(),
        P(),
        P(),
        P(("space", "chaos")),
        P(("space", "chaos")),
        P(("space", "chaos")),
        P(("space", "chaos")),
        P(("space", "chaos"), None),
        P(("space", "chaos"), None),
        P(("space", "chaos"), None),
        P(("space", "chaos")),
        P(("space", "chaos")),
    )
    out_specs = P("chaos", "space")
    return jax.shard_map(local, mesh=mesh, in_specs=in_specs, out_specs=out_specs, check_vma=False)
```

```python
import functools

import jax
import jax.numpy as jnp
import numpy as np
from jax import lax
from jax.experimental import pallas as pl
from jax.experimental.pallas import tpu as pltpu
from jax.sharding import PartitionSpec as P

ELEM_NODES = 64
LANES = 128
FACE = 16
VMEM_LIMIT = 56 * 1024 * 1024
NT = (((1,), (1,)), ((), ()))
NN = (((1,), (0,)), ((), ()))


def face_nodes():
    node_rows = []
    for side_idx in range(6):
        normal_axis = side_idx // 2
        plane_level = 3 * (side_idx % 2)
        row_nodes = []
        for first_coord in range(4):
            for second_coord in range(4):
                position = [first_coord, second_coord]
                position.insert(normal_axis, plane_level)
                row_nodes.append(16 * position[0] + 4 * position[1] + position[2])
        node_rows.append(row_nodes)
    return np.array(node_rows, dtype=np.int32)


def side_nodes(side_ids):
    node_table = jnp.asarray(face_nodes())
    side_hot = (side_ids[:, None] == jnp.arange(6, dtype=jnp.int32)[None, :]).astype(jnp.int32)
    return jnp.sum(side_hot[:, :, None] * node_table[None, :, :], axis=1)


def mm(a, b, dims=NN):
    return lax.dot_general(a, b, dims, preferred_element_type=jnp.float32)


def iota(shape, dim):
    return lax.broadcasted_iota(jnp.int32, shape, dim)


def hot(mask):
    return jnp.where(mask, 1.0, 0.0).astype(jnp.bfloat16)


def perm_hot(shape, chaos_dim, wide_dim, part, padded):
    i = iota(shape, chaos_dim)
    return hot(iota(shape, wide_dim) == i // part * padded + i % part)


def block_diag(flat):
    spread = mm(hot(iota((LANES, 8), 0) // FACE == iota((LANES, 8), 1)), flat)
    own_row = iota((LANES, 256), 1) // FACE == iota((LANES, 256), 0) % FACE
    spread = jnp.where(own_row, spread, 0.0).astype(jnp.bfloat16)
    fold = hot(iota((256, LANES), 0) % FACE == iota((256, LANES), 1) % FACE)
    tiled = mm(spread, fold)
    same = iota((LANES, LANES), 0) // FACE == iota((LANES, LANES), 1) // FACE
    return jnp.where(same, tiled, 0.0).astype(jnp.bfloat16)


def node_hot(target_row):
    return hot(iota((8 * LANES, LANES), 0) == target_row)


def faces_of(fp_ref, pair_ref, group):
    return jnp.concatenate([fp_ref[pair_ref[group * 8 + j]] for j in range(8)], axis=1)


def weave_kernel(mort_ref, target_ref, out_ref):
    for h in range(out_ref.shape[0]):
        mats = block_diag(mort_ref[h])
        out_ref[h] = mm(mats, node_hot(target_ref[h]), NT).astype(jnp.bfloat16)


def tail_hot(shape, dense_dim, low):
    dense, row = iota(shape, dense_dim), iota(shape, 1 - dense_dim)
    return hot((row // 16 == dense // low) & (row % 16 == dense % low))


def send_kernel(field_ref, out_ref):
    part, nodes = field_ref.shape
    high = part // 16 * 16
    low, width = part - high, nodes // 16
    total = jnp.zeros((16 * low, width), jnp.float32)
    for q in range(16):
        cols = slice(q * width, (q + 1) * width)
        out_ref[0, q * high:(q + 1) * high, :] = field_ref[:high, cols]
        shape = (16 * low, low)
        place = hot(iota(shape, 0) == q * low + iota(shape, 1))
        total = total + mm(place, field_ref[high:part, cols])
    out_ref[0, 16 * high:, :] = total.astype(jnp.bfloat16)


def receive_kernel(in_ref, out_ref):
    part, nodes = out_ref.shape
    high = part // 16 * 16
    low, width = part - high, nodes // 16
    tail = in_ref[0, 16 * high:, :]
    for q in range(16):
        cols = slice(q * width, (q + 1) * width)
        out_ref[:high, cols] = in_ref[0, q * high:(q + 1) * high, :]
        shape = (low, 16 * low)
        pick = hot(iota(shape, 1) == q * low + iota(shape, 0))
        out_ref[high:part, cols] = mm(pick, tail).astype(jnp.bfloat16)


def pack_kernel(owner_col_ref, owner_row_ref, die_ref, int_ref, small_ref, die_out, meta_out, small_out, *, cap):
    segs = owner_row_ref.shape[1]
    slots = die_out.shape[0]
    same = owner_col_ref[...] == owner_row_ref[...]
    before = iota((segs, segs), 0) < iota((segs, segs), 1)
    rank = jnp.sum(jnp.where(same & before, 1.0, 0.0), axis=0, keepdims=True).astype(jnp.int32)
    place = hot(iota((slots, segs), 0) == owner_row_ref[...] * cap + rank)
    die_out[...] = mm(place, die_ref[...]).astype(jnp.bfloat16)
    small = mm(place, small_ref[...])
    small_out[...] = small
    meta_out[:, :256] = mm(place, int_ref[...]).astype(jnp.bfloat16)
    meta_out[:, 256:] = small.astype(jnp.bfloat16)


def unpack(wide_ref, fp_out, part):
    n_chaos, rows, width = wide_ref.shape
    high = part // 16 * 16
    low = part - high
    padded = high + 16
    spread = tail_hot((256, 16 * low), 1, low)
    tails = [mm(spread, wide_ref[c, 16 * high:, :]).astype(jnp.bfloat16) for c in range(n_chaos)]
    perm = perm_hot((part * n_chaos, padded * n_chaos), 0, 1, part, padded)
    per = width // LANES
    for q in range(16):
        pieces = []
        for c in range(n_chaos):
            pieces.append(wide_ref[c, q * high:(q + 1) * high, :])
            pieces.append(tails[c][q * 16:(q + 1) * 16])
        block = mm(perm, jnp.concatenate(pieces, axis=0)).astype(jnp.bfloat16)
        for h in range(per):
            fp_out[q * per + h] = block[:, h * LANES:(h + 1) * LANES]


def project_kernel(pair_ref, wide_ref, weave_ref, fp_out, proj_out, *, part):
    step = pl.program_id(0)

    @pl.when(step == 0)
    def _():
        unpack(wide_ref, fp_out, part)

    for h in range(proj_out.shape[0]):
        face = faces_of(fp_out, pair_ref, step * proj_out.shape[0] + h)
        proj_out[h] = mm(face, weave_ref[h], NT).astype(jnp.bfloat16)


def own_project_kernel(pair_ref, fp_ref, weave_ref, proj_out):
    for h in range(proj_out.shape[0]):
        face = faces_of(fp_ref, pair_ref, pl.program_id(0) * proj_out.shape[0] + h)
        proj_out[h] = mm(face, weave_ref[h], NT)


def mix(coupling_ref, block, weights):
    total = weights[0:1] * block.astype(jnp.float32)
    for k in range(coupling_ref.shape[0]):
        total = total + weights[k + 1:k + 2] * mm(coupling_ref[k], block)
    return total.astype(jnp.bfloat16)


def element_kernel(fp_ref, coupling_ref, kl_ref, stiff_ref, out_ref):
    def step(p, carry):
        block = jnp.concatenate([fp_ref[2 * p], fp_ref[2 * p + 1]], axis=1)
        mixed = mix(coupling_ref, block, kl_ref[p])
        out_ref[2 * p] = mm(mixed[:, :LANES], stiff_ref[2 * p], NT)
        out_ref[2 * p + 1] = mm(mixed[:, LANES:], stiff_ref[2 * p + 1], NT)
        return carry

    lax.fori_loop(0, fp_ref.shape[0] // 2, step, 0)


def flux_kernel(recv_ref, own_ref, coupling_ref, coef_ref, flux_out):
    def step(p, carry):
        jump = [
            (recv_ref[2 * p + h].astype(jnp.float32) - own_ref[2 * p + h]).astype(jnp.bfloat16)
            for h in range(2)
        ]
        flux = mix(coupling_ref, jnp.concatenate(jump, axis=1), coef_ref[p])
        flux_out[2 * p] = flux[:, :LANES]
        flux_out[2 * p + 1] = flux[:, LANES:]
        return carry

    lax.fori_loop(0, recv_ref.shape[0] // 2, step, 0)


def scatter_step(pair_ref, flux_ref, weave_ref, acc_ref, sign):
    for h in range(flux_ref.shape[0]):
        back = mm(flux_ref[h], weave_ref[h])
        for j in range(8):
            pair = pair_ref[(pl.program_id(0) * flux_ref.shape[0] + h) * 8 + j]
            acc_ref[pair] = acc_ref[pair] + sign * back[:, j * LANES:(j + 1) * LANES]


def own_back_kernel(pair_ref, flux_ref, weave_ref, start_ref, acc_out):
    @pl.when(pl.program_id(0) == 0)
    def _():
        acc_out[...] = start_ref[...]

    scatter_step(pair_ref, flux_ref, weave_ref, acc_out, -1.0)


def die_back_kernel(pair_ref, flux_ref, weave_ref, start_ref, out_ref, acc_ref, tail_ref, *, part):
    @pl.when(pl.program_id(0) == 0)
    def _():
        acc_ref[...] = start_ref[...]

    scatter_step(pair_ref, flux_ref, weave_ref, acc_ref, 1.0)

    @pl.when(pl.program_id(0) == pl.num_programs(0) - 1)
    def _():
        n_chaos, rows, width = out_ref.shape
        high = part // 16 * 16
        low = part - high
        padded = high + 16
        perm = perm_hot((padded * n_chaos, part * n_chaos), 1, 0, part, padded)
        per = width // LANES
        for q in range(16):
            block = jnp.concatenate([acc_ref[q * per + h].astype(jnp.bfloat16) for h in range(per)], axis=1)
            block = mm(perm, block).astype(jnp.bfloat16)
            for c in range(n_chaos):
                out_ref[c, q * high:(q + 1) * high, :] = block[c * padded:c * padded + high]
                tail_ref[c, q * 16:(q + 1) * 16, :] = block[c * padded + high:(c + 1) * padded]
        gather = tail_hot((16 * low, 256), 0, low)
        for c in range(n_chaos):
            out_ref[c, 16 * high:, :] = mm(gather, tail_ref[c]).astype(jnp.bfloat16)


def call(kernel, outs, args, scalars=0, scratch=(), steps=0, split=(), split_outs=()):
    many = isinstance(outs, tuple)
    shapes = outs if many else (outs,)

    def spec(shape, cut):
        if steps == 0:
            return pl.BlockSpec(memory_space=pltpu.VMEM)
        rest = (0,) * (len(shape) - 1)
        if cut:
            return pl.BlockSpec((shape[0] // steps,) + tuple(shape[1:]), lambda i: (i,) + rest)
        return pl.BlockSpec(tuple(shape), lambda i: (0,) + rest)

    in_specs = [
        pl.BlockSpec(memory_space=pltpu.SMEM) if n < scalars else spec(x.shape, n in split)
        for n, x in enumerate(args)
    ]
    out_specs = tuple(spec(x.shape, n in split_outs) for n, x in enumerate(shapes))
    moved = sum(x.size * x.dtype.itemsize for x in (*args, *shapes))
    result = pl.pallas_call(
        kernel,
        out_shape=shapes,
        grid=(steps,) if steps else (),
        in_specs=in_specs,
        out_specs=out_specs,
        scratch_shapes=scratch,
        compiler_params=pltpu.CompilerParams(vmem_limit_bytes=VMEM_LIMIT),
        cost_estimate=pl.CostEstimate(flops=0, bytes_accessed=moved, transcendentals=0),
    )(*args)
    return result if many else result[0]


def dense_coupling(triple_mode, triple_row, triple_col, triple_value, mode_count, chaos_width):
    flat_index = triple_mode * chaos_width + triple_row
    left_hot = (
        flat_index[:, None] == jnp.arange(mode_count * chaos_width, dtype=jnp.int32)[None, :]
    ).astype(jnp.float32)
    right_hot = (triple_col[:, None] == jnp.arange(chaos_width, dtype=jnp.int32)[None, :]).astype(
        jnp.float32
    ) * triple_value[:, None]
    summed = jnp.einsum(
        "ta,tb->ab",
        left_hot,
        right_hot,
        precision=lax.Precision.HIGHEST,
        preferred_element_type=jnp.float32,
    )
    return summed.reshape(mode_count, chaos_width, chaos_width).astype(jnp.bfloat16)


def slot_targets(elem, side):
    slots = elem.shape[0]
    lane_block = (jnp.arange(slots, dtype=jnp.int32) % 8) * LANES + (elem % 2) * ELEM_NODES
    target = lane_block[:, None] + side_nodes(side)
    return elem // 2, target.reshape(slots // 8, 1, LANES)


def lane_weights(rows, repeat):
    rows = jnp.pad(rows, ((0, 16 - rows.shape[0]), (0, 0)))
    per = 256 // repeat
    tiles = rows.shape[1] // per
    rows = jnp.transpose(rows.reshape(16, tiles, per), (1, 0, 2))
    spread = (jnp.arange(per)[:, None] == jnp.arange(256)[None, :] // repeat).astype(jnp.float32)
    return jnp.einsum("tkp,pl->tkl", rows, spread, precision=lax.Precision.HIGHEST)


def local(
    field,
    stiffness,
    kl_coef,
    triple_mode,
    triple_row,
    triple_col,
    triple_value,
    die_elem,
    die_side,
    seg_owner,
    seg_face,
    die_mortar,
    int_mortar,
    bump_coef,
    int_elem,
    int_side,
):
    n_chaos = lax.axis_size("chaos")
    devices = lax.axis_size("space") * n_chaos
    part, local_nodes = field.shape
    chaos = part * n_chaos
    nodes = local_nodes // n_chaos
    segs = die_elem.shape[0]
    cap = max(2, 2 * segs // devices)
    slots = devices * cap
    groups = slots // 8
    pairs = nodes // LANES
    modes = bump_coef.shape[1] - 1
    bf16, f32 = jnp.bfloat16, jnp.float32
    axes = ("space", "chaos")

    sent = pl.pallas_call(
        send_kernel,
        out_shape=jax.ShapeDtypeStruct((n_chaos, 16 * part, nodes // 16), bf16),
        grid=(n_chaos,),
        in_specs=[pl.BlockSpec((part, nodes), lambda c: (0, c))],
        out_specs=pl.BlockSpec((1, 16 * part, nodes // 16), lambda c: (c, 0, 0)),
    )(field)
    wide = lax.all_to_all(sent, "chaos", split_axis=0, concat_axis=0, tiled=True)

    ints = jnp.stack([seg_face, die_elem, die_side], axis=1).astype(bf16)
    small = jnp.pad(jnp.concatenate([bump_coef, ints], axis=1), ((0, 0), (0, LANES - modes - 4)))
    die_slots, meta, small_slots = call(
        functools.partial(pack_kernel, cap=cap),
        (
            jax.ShapeDtypeStruct((slots, 256), bf16),
            jax.ShapeDtypeStruct((slots, 256 + LANES), bf16),
            jax.ShapeDtypeStruct((slots, LANES), f32),
        ),
        (seg_owner[:, None], seg_owner[None, :], die_mortar, int_mortar, small),
    )
    die_ids = small_slots[:, modes + 2:modes + 4].astype(jnp.int32)
    die_pair, die_target = slot_targets(die_ids[:, 0], die_ids[:, 1])

    coupling = dense_coupling(triple_mode, triple_row, triple_col, triple_value, modes, chaos)
    kl_lanes = lane_weights(kl_coef, ELEM_NODES)
    blocks = stiffness.reshape(pairs, 2, ELEM_NODES, 1, ELEM_NODES)
    on_diag = jnp.eye(2, dtype=bool)[None, :, None, :, None]
    stiff = jnp.where(on_diag, blocks, jnp.zeros((), bf16)).reshape(pairs, LANES, LANES)

    groups3 = (groups, 8, 256)
    weave_shape = jax.ShapeDtypeStruct((groups, LANES, 8 * LANES), bf16)
    steps = groups // 4
    die_weave = call(
        weave_kernel,
        weave_shape,
        (die_slots.reshape(groups3), die_target),
        steps=steps,
        split=(0, 1),
        split_outs=(0,),
    )
    wide, meta, die_weave, die_pair, coupling, kl_lanes, stiff = lax.optimization_barrier(
        (wide, meta, die_weave, die_pair, coupling, kl_lanes, stiff)
    )
    meta = lax.all_to_all(meta, axes, split_axis=0, concat_axis=0, tiled=True)
    fp, proj = call(
        functools.partial(project_kernel, part=part),
        (
            jax.ShapeDtypeStruct((pairs, chaos, LANES), bf16),
            jax.ShapeDtypeStruct((groups, chaos, LANES), bf16),
        ),
        (die_pair, wide, die_weave),
        1,
        steps=steps,
        split=(2,),
        split_outs=(1,),
    )

    meta, proj = lax.optimization_barrier((meta, proj))

    def exchange(values):
        per = devices // groups
        values = values.reshape(groups, chaos, per, LANES // per)
        values = jnp.transpose(values, (0, 2, 1, 3)).reshape(devices, chaos, LANES // per)
        values = lax.all_to_all(values, axes, split_axis=0, concat_axis=0, tiled=True)
        values = values.reshape(groups, per, chaos, LANES // per)
        return jnp.transpose(values, (0, 2, 1, 3)).reshape(groups, chaos, LANES)

    recv = exchange(proj)

    int_slots = meta[:, :256]
    recv_small = meta[:, 256:256 + modes + 2].astype(f32)
    coef_lanes = lane_weights(recv_small[:, :modes + 1].T, FACE)
    face_hot = recv_small[:, modes + 1].astype(jnp.int32)[:, None] == jnp.arange(int_elem.shape[0])[None, :]
    own_elem = jnp.sum(jnp.where(face_hot, int_elem[None, :], 0), axis=1)
    own_side = jnp.sum(jnp.where(face_hot, int_side[None, :], 0), axis=1)
    own_pair, own_target = slot_targets(own_elem, own_side)

    int_weave = call(
        weave_kernel,
        weave_shape,
        (int_slots.reshape(groups3), own_target),
        steps=steps,
        split=(0, 1),
        split_outs=(0,),
    )
    local_out = call(
        element_kernel,
        jax.ShapeDtypeStruct((pairs, chaos, LANES), f32),
        (fp, coupling, kl_lanes, stiff),
    )
    own_proj = call(
        own_project_kernel,
        jax.ShapeDtypeStruct((groups, chaos, LANES), f32),
        (own_pair, fp, int_weave),
        1,
        steps=steps,
        split=(2,),
        split_outs=(0,),
    )
    flux = call(
        flux_kernel,
        jax.ShapeDtypeStruct((groups, chaos, LANES), bf16),
        (recv, own_proj, coupling, coef_lanes),
    )
    back_flux = exchange(flux)
    local_out = call(
        own_back_kernel,
        jax.ShapeDtypeStruct((pairs, chaos, LANES), f32),
        (own_pair, flux, int_weave, local_out),
        1,
        steps=steps,
        split=(1, 2),
    )
    result = call(
        functools.partial(die_back_kernel, part=part),
        jax.ShapeDtypeStruct(sent.shape, bf16),
        (die_pair, back_flux, die_weave, local_out),
        1,
        (
            pltpu.VMEM((pairs, chaos, LANES), f32),
            pltpu.VMEM((n_chaos, 256, nodes // 16), bf16),
        ),
        steps=steps,
        split=(1, 2),
    )
    returned = lax.all_to_all(result, "chaos", split_axis=0, concat_axis=0, tiled=True)
    return pl.pallas_call(
        receive_kernel,
        out_shape=jax.ShapeDtypeStruct((part, local_nodes), bf16),
        grid=(n_chaos,),
        in_specs=[pl.BlockSpec((1, 16 * part, nodes // 16), lambda c: (c, 0, 0))],
        out_specs=pl.BlockSpec((part, nodes), lambda c: (0, c)),
    )(returned)


def solution(mesh):
    in_specs = (
        P("chaos", "space"),
        P(("space", "chaos"), None),
        P(None, ("space", "chaos")),
        P(),
        P(),
        P(),
        P(),
        P(("space", "chaos")),
        P(("space", "chaos")),
        P(("space", "chaos")),
        P(("space", "chaos")),
        P(("space", "chaos"), None),
        P(("space", "chaos"), None),
        P(("space", "chaos"), None),
        P(("space", "chaos")),
        P(("space", "chaos")),
    )
    out_specs = P("chaos", "space")
    return jax.shard_map(local, mesh=mesh, in_specs=in_specs, out_specs=out_specs, check_vma=False)
```

```python
import functools

import jax
import jax.numpy as jnp
import numpy as np
from jax import lax
from jax.experimental import pallas as pl
from jax.experimental.pallas import tpu as pltpu
from jax.sharding import PartitionSpec as P

ELEM_NODES = 64
LANES = 128
FACE = 16
VMEM_LIMIT = 56 * 1024 * 1024
NT = (((1,), (1,)), ((), ()))
NN = (((1,), (0,)), ((), ()))


def face_nodes():
    node_rows = []
    for side_idx in range(6):
        normal_axis = side_idx // 2
        plane_level = 3 * (side_idx % 2)
        row_nodes = []
        for first_coord in range(4):
            for second_coord in range(4):
                position = [first_coord, second_coord]
                position.insert(normal_axis, plane_level)
                row_nodes.append(16 * position[0] + 4 * position[1] + position[2])
        node_rows.append(row_nodes)
    return np.array(node_rows, dtype=np.int32)


def side_nodes(side_ids):
    node_table = jnp.asarray(face_nodes())
    side_hot = (side_ids[:, None] == jnp.arange(6, dtype=jnp.int32)[None, :]).astype(jnp.int32)
    return jnp.sum(side_hot[:, :, None] * node_table[None, :, :], axis=1)


def mm(a, b, dims=NN):
    return lax.dot_general(a, b, dims, preferred_element_type=jnp.float32)


def iota(shape, dim):
    return lax.broadcasted_iota(jnp.int32, shape, dim)


def hot(mask):
    return jnp.where(mask, 1.0, 0.0).astype(jnp.bfloat16)


def perm_hot(shape, chaos_dim, wide_dim, part, padded):
    i = iota(shape, chaos_dim)
    return hot(iota(shape, wide_dim) == i // part * padded + i % part)


def block_diag(flat):
    spread = mm(hot(iota((LANES, 8), 0) // FACE == iota((LANES, 8), 1)), flat)
    own_row = iota((LANES, 256), 1) // FACE == iota((LANES, 256), 0) % FACE
    spread = jnp.where(own_row, spread, 0.0).astype(jnp.bfloat16)
    fold = hot(iota((256, LANES), 0) % FACE == iota((256, LANES), 1) % FACE)
    tiled = mm(spread, fold)
    same = iota((LANES, LANES), 0) // FACE == iota((LANES, LANES), 1) // FACE
    return jnp.where(same, tiled, 0.0).astype(jnp.bfloat16)


def node_hot(target_row):
    return hot(iota((8 * LANES, LANES), 0) == target_row)


def faces_of(fp_ref, pair_ref, group):
    return jnp.concatenate([fp_ref[pair_ref[group * 8 + j]] for j in range(8)], axis=1)


def weave_kernel(mort_ref, target_ref, out_ref):
    for h in range(out_ref.shape[0]):
        mats = block_diag(mort_ref[h])
        out_ref[h] = mm(mats, node_hot(target_ref[h]), NT).astype(jnp.bfloat16)


def tail_hot(shape, dense_dim, low):
    dense, row = iota(shape, dense_dim), iota(shape, 1 - dense_dim)
    return hot((row // 16 == dense // low) & (row % 16 == dense % low))


def send_kernel(field_ref, out_ref):
    part, nodes = field_ref.shape
    high = part // 16 * 16
    low, width = part - high, nodes // 16
    total = jnp.zeros((16 * low, width), jnp.float32)
    for q in range(16):
        cols = slice(q * width, (q + 1) * width)
        out_ref[0, q * high:(q + 1) * high, :] = field_ref[:high, cols]
        shape = (16 * low, low)
        place = hot(iota(shape, 0) == q * low + iota(shape, 1))
        total = total + mm(place, field_ref[high:part, cols])
    out_ref[0, 16 * high:, :] = total.astype(jnp.bfloat16)


def receive_kernel(in_ref, out_ref):
    part, nodes = out_ref.shape
    high = part // 16 * 16
    low, width = part - high, nodes // 16
    tail = in_ref[0, 16 * high:, :]
    for q in range(16):
        cols = slice(q * width, (q + 1) * width)
        out_ref[:high, cols] = in_ref[0, q * high:(q + 1) * high, :]
        shape = (low, 16 * low)
        pick = hot(iota(shape, 1) == q * low + iota(shape, 0))
        out_ref[high:part, cols] = mm(pick, tail).astype(jnp.bfloat16)


def pack_kernel(owner_col_ref, owner_row_ref, die_ref, int_ref, small_ref, die_out, meta_out, small_out, *, cap):
    segs = owner_row_ref.shape[1]
    slots = die_out.shape[0]
    same = owner_col_ref[...] == owner_row_ref[...]
    before = iota((segs, segs), 0) < iota((segs, segs), 1)
    rank = jnp.sum(jnp.where(same & before, 1.0, 0.0), axis=0, keepdims=True).astype(jnp.int32)
    place = hot(iota((slots, segs), 0) == owner_row_ref[...] * cap + rank)
    die_out[...] = mm(place, die_ref[...]).astype(jnp.bfloat16)
    small = mm(place, small_ref[...])
    small_out[...] = small
    meta_out[:, :256] = mm(place, int_ref[...]).astype(jnp.bfloat16)
    meta_out[:, 256:] = small.astype(jnp.bfloat16)


def unpack(wide_ref, fp_out, part):
    n_chaos, rows, width = wide_ref.shape
    high = part // 16 * 16
    low = part - high
    padded = high + 16
    spread = tail_hot((256, 16 * low), 1, low)
    tails = [mm(spread, wide_ref[c, 16 * high:, :]).astype(jnp.bfloat16) for c in range(n_chaos)]
    perm = perm_hot((part * n_chaos, padded * n_chaos), 0, 1, part, padded)
    per = width // LANES
    for q in range(16):
        pieces = []
        for c in range(n_chaos):
            pieces.append(wide_ref[c, q * high:(q + 1) * high, :])
            pieces.append(tails[c][q * 16:(q + 1) * 16])
        block = mm(perm, jnp.concatenate(pieces, axis=0)).astype(jnp.bfloat16)
        for h in range(per):
            fp_out[q * per + h] = block[:, h * LANES:(h + 1) * LANES]


def project_kernel(pair_ref, wide_ref, weave_ref, fp_out, proj_out, *, part):
    step = pl.program_id(0)

    @pl.when(step == 0)
    def _():
        unpack(wide_ref, fp_out, part)

    for h in range(proj_out.shape[0]):
        face = faces_of(fp_out, pair_ref, step * proj_out.shape[0] + h)
        proj_out[h] = mm(face, weave_ref[h], NT).astype(jnp.bfloat16)


def own_project_kernel(pair_ref, fp_ref, weave_ref, proj_out):
    for h in range(proj_out.shape[0]):
        face = faces_of(fp_ref, pair_ref, pl.program_id(0) * proj_out.shape[0] + h)
        proj_out[h] = mm(face, weave_ref[h], NT)


def mix(coupling_ref, block, weights):
    total = weights[0:1] * block.astype(jnp.float32)
    for k in range(coupling_ref.shape[0]):
        total = total + weights[k + 1:k + 2] * mm(coupling_ref[k], block)
    return total.astype(jnp.bfloat16)


def element_kernel(fp_ref, coupling_ref, kl_ref, stiff_ref, out_ref):
    def step(p, carry):
        block = jnp.concatenate([fp_ref[2 * p], fp_ref[2 * p + 1]], axis=1)
        mixed = mix(coupling_ref, block, kl_ref[p])
        out_ref[2 * p] = mm(mixed[:, :LANES], stiff_ref[2 * p], NT)
        out_ref[2 * p + 1] = mm(mixed[:, LANES:], stiff_ref[2 * p + 1], NT)
        return carry

    lax.fori_loop(0, fp_ref.shape[0] // 2, step, 0)


def flux_kernel(recv_ref, own_ref, coupling_ref, coef_ref, flux_out):
    def step(p, carry):
        jump = [
            (recv_ref[2 * p + h].astype(jnp.float32) - own_ref[2 * p + h]).astype(jnp.bfloat16)
            for h in range(2)
        ]
        flux = mix(coupling_ref, jnp.concatenate(jump, axis=1), coef_ref[p])
        flux_out[2 * p] = flux[:, :LANES]
        flux_out[2 * p + 1] = flux[:, LANES:]
        return carry

    lax.fori_loop(0, recv_ref.shape[0] // 2, step, 0)


def scatter_step(pair_ref, flux_ref, weave_ref, acc_ref, sign):
    for h in range(flux_ref.shape[0]):
        back = mm(flux_ref[h], weave_ref[h])
        for j in range(8):
            pair = pair_ref[(pl.program_id(0) * flux_ref.shape[0] + h) * 8 + j]
            acc_ref[pair] = acc_ref[pair] + sign * back[:, j * LANES:(j + 1) * LANES]


def own_back_kernel(pair_ref, flux_ref, weave_ref, start_ref, acc_out):
    @pl.when(pl.program_id(0) == 0)
    def _():
        acc_out[...] = start_ref[...]

    scatter_step(pair_ref, flux_ref, weave_ref, acc_out, -1.0)


def die_back_kernel(pair_ref, flux_ref, weave_ref, start_ref, out_ref, acc_ref, tail_ref, *, part):
    @pl.when(pl.program_id(0) == 0)
    def _():
        acc_ref[...] = start_ref[...]

    scatter_step(pair_ref, flux_ref, weave_ref, acc_ref, 1.0)

    @pl.when(pl.program_id(0) == pl.num_programs(0) - 1)
    def _():
        n_chaos, rows, width = out_ref.shape
        high = part // 16 * 16
        low = part - high
        padded = high + 16
        perm = perm_hot((padded * n_chaos, part * n_chaos), 1, 0, part, padded)
        per = width // LANES
        for q in range(16):
            block = jnp.concatenate([acc_ref[q * per + h].astype(jnp.bfloat16) for h in range(per)], axis=1)
            block = mm(perm, block).astype(jnp.bfloat16)
            for c in range(n_chaos):
                out_ref[c, q * high:(q + 1) * high, :] = block[c * padded:c * padded + high]
                tail_ref[c, q * 16:(q + 1) * 16, :] = block[c * padded + high:(c + 1) * padded]
        gather = tail_hot((16 * low, 256), 0, low)
        for c in range(n_chaos):
            out_ref[c, 16 * high:, :] = mm(gather, tail_ref[c]).astype(jnp.bfloat16)


def call(kernel, outs, args, scalars=0, scratch=(), steps=0, split=(), split_outs=()):
    many = isinstance(outs, tuple)
    shapes = outs if many else (outs,)

    def spec(shape, cut):
        if steps == 0:
            return pl.BlockSpec(memory_space=pltpu.VMEM)
        rest = (0,) * (len(shape) - 1)
        if cut:
            return pl.BlockSpec((shape[0] // steps,) + tuple(shape[1:]), lambda i: (i,) + rest)
        return pl.BlockSpec(tuple(shape), lambda i: (0,) + rest)

    in_specs = [
        pl.BlockSpec(memory_space=pltpu.SMEM) if n < scalars else spec(x.shape, n in split)
        for n, x in enumerate(args)
    ]
    out_specs = tuple(spec(x.shape, n in split_outs) for n, x in enumerate(shapes))
    moved = sum(x.size * x.dtype.itemsize for x in (*args, *shapes))
    result = pl.pallas_call(
        kernel,
        out_shape=shapes,
        grid=(steps,) if steps else (),
        in_specs=in_specs,
        out_specs=out_specs,
        scratch_shapes=scratch,
        compiler_params=pltpu.CompilerParams(vmem_limit_bytes=VMEM_LIMIT),
        cost_estimate=pl.CostEstimate(flops=0, bytes_accessed=moved, transcendentals=0),
    )(*args)
    return result if many else result[0]


def dense_coupling(triple_mode, triple_row, triple_col, triple_value, mode_count, chaos_width):
    flat_index = triple_mode * chaos_width + triple_row
    left_hot = (
        flat_index[:, None] == jnp.arange(mode_count * chaos_width, dtype=jnp.int32)[None, :]
    ).astype(jnp.float32)
    right_hot = (triple_col[:, None] == jnp.arange(chaos_width, dtype=jnp.int32)[None, :]).astype(
        jnp.float32
    ) * triple_value[:, None]
    summed = jnp.einsum(
        "ta,tb->ab",
        left_hot,
        right_hot,
        precision=lax.Precision.HIGHEST,
        preferred_element_type=jnp.float32,
    )
    return summed.reshape(mode_count, chaos_width, chaos_width).astype(jnp.bfloat16)


def slot_targets(elem, side):
    slots = elem.shape[0]
    lane_block = (jnp.arange(slots, dtype=jnp.int32) % 8) * LANES + (elem % 2) * ELEM_NODES
    target = lane_block[:, None] + side_nodes(side)
    return elem // 2, target.reshape(slots // 8, 1, LANES)


def lane_weights(rows, repeat):
    rows = jnp.pad(rows, ((0, 16 - rows.shape[0]), (0, 0)))
    per = 256 // repeat
    tiles = rows.shape[1] // per
    rows = jnp.transpose(rows.reshape(16, tiles, per), (1, 0, 2))
    spread = (jnp.arange(per)[:, None] == jnp.arange(256)[None, :] // repeat).astype(jnp.float32)
    return jnp.einsum("tkp,pl->tkl", rows, spread, precision=lax.Precision.HIGHEST)


def local(
    field,
    stiffness,
    kl_coef,
    triple_mode,
    triple_row,
    triple_col,
    triple_value,
    die_elem,
    die_side,
    seg_owner,
    seg_face,
    die_mortar,
    int_mortar,
    bump_coef,
    int_elem,
    int_side,
):
    n_chaos = lax.axis_size("chaos")
    devices = lax.axis_size("space") * n_chaos
    part, local_nodes = field.shape
    chaos = part * n_chaos
    nodes = local_nodes // n_chaos
    segs = die_elem.shape[0]
    cap = max(2, 2 * segs // devices)
    slots = devices * cap
    groups = slots // 8
    pairs = nodes // LANES
    modes = bump_coef.shape[1] - 1
    bf16, f32 = jnp.bfloat16, jnp.float32
    axes = ("space", "chaos")

    sent = pl.pallas_call(
        send_kernel,
        out_shape=jax.ShapeDtypeStruct((n_chaos, 16 * part, nodes // 16), bf16),
        grid=(n_chaos,),
        in_specs=[pl.BlockSpec((part, nodes), lambda c: (0, c))],
        out_specs=pl.BlockSpec((1, 16 * part, nodes // 16), lambda c: (c, 0, 0)),
    )(field)
    wide = lax.all_to_all(sent, "chaos", split_axis=0, concat_axis=0, tiled=True)

    ints = jnp.stack([seg_face, die_elem, die_side], axis=1).astype(bf16)
    small = jnp.pad(jnp.concatenate([bump_coef, ints], axis=1), ((0, 0), (0, LANES - modes - 4)))
    die_slots, meta, small_slots = call(
        functools.partial(pack_kernel, cap=cap),
        (
            jax.ShapeDtypeStruct((slots, 256), bf16),
            jax.ShapeDtypeStruct((slots, 256 + LANES), bf16),
            jax.ShapeDtypeStruct((slots, LANES), f32),
        ),
        (seg_owner[:, None], seg_owner[None, :], die_mortar, int_mortar, small),
    )
    die_ids = small_slots[:, modes + 2:modes + 4].astype(jnp.int32)
    die_pair, die_target = slot_targets(die_ids[:, 0], die_ids[:, 1])

    coupling = dense_coupling(triple_mode, triple_row, triple_col, triple_value, modes, chaos)
    groups3 = (groups, 8, 256)
    weave_shape = jax.ShapeDtypeStruct((groups, LANES, 8 * LANES), bf16)
    steps = groups // 4
    die_weave = call(
        weave_kernel,
        weave_shape,
        (die_slots.reshape(groups3), die_target),
        steps=steps,
        split=(0, 1),
        split_outs=(0,),
    )
    wide, meta, die_weave, die_pair, coupling = lax.optimization_barrier(
        (wide, meta, die_weave, die_pair, coupling)
    )
    meta = lax.all_to_all(meta, axes, split_axis=0, concat_axis=0, tiled=True)
    fp, proj = call(
        functools.partial(project_kernel, part=part),
        (
            jax.ShapeDtypeStruct((pairs, chaos, LANES), bf16),
            jax.ShapeDtypeStruct((groups, chaos, LANES), bf16),
        ),
        (die_pair, wide, die_weave),
        1,
        steps=steps,
        split=(2,),
        split_outs=(1,),
    )

    meta, proj = lax.optimization_barrier((meta, proj))

    def exchange(values):
        per = devices // groups
        values = values.reshape(groups, chaos, per, LANES // per)
        values = jnp.transpose(values, (0, 2, 1, 3)).reshape(devices, chaos, LANES // per)
        values = lax.all_to_all(values, axes, split_axis=0, concat_axis=0, tiled=True)
        values = values.reshape(groups, per, chaos, LANES // per)
        return jnp.transpose(values, (0, 2, 1, 3)).reshape(groups, chaos, LANES)

    recv = exchange(proj)

    int_slots = meta[:, :256]
    recv_small = meta[:, 256:256 + modes + 2].astype(f32)
    coef_lanes = lane_weights(recv_small[:, :modes + 1].T, FACE)
    face_hot = recv_small[:, modes + 1].astype(jnp.int32)[:, None] == jnp.arange(int_elem.shape[0])[None, :]
    own_elem = jnp.sum(jnp.where(face_hot, int_elem[None, :], 0), axis=1)
    own_side = jnp.sum(jnp.where(face_hot, int_side[None, :], 0), axis=1)
    own_pair, own_target = slot_targets(own_elem, own_side)

    int_weave = call(
        weave_kernel,
        weave_shape,
        (int_slots.reshape(groups3), own_target),
        steps=steps,
        split=(0, 1),
        split_outs=(0,),
    )
    own_proj = call(
        own_project_kernel,
        jax.ShapeDtypeStruct((groups, chaos, LANES), f32),
        (own_pair, fp, int_weave),
        1,
        steps=steps,
        split=(2,),
        split_outs=(0,),
    )
    flux = call(
        flux_kernel,
        jax.ShapeDtypeStruct((groups, chaos, LANES), bf16),
        (recv, own_proj, coupling, coef_lanes),
    )
    flux, stiffness, kl_coef = lax.optimization_barrier((flux, stiffness, kl_coef))
    back_flux = exchange(flux)
    kl_lanes = lane_weights(kl_coef, ELEM_NODES)
    blocks = stiffness.reshape(pairs, 2, ELEM_NODES, 1, ELEM_NODES)
    on_diag = jnp.eye(2, dtype=bool)[None, :, None, :, None]
    stiff = jnp.where(on_diag, blocks, jnp.zeros((), bf16)).reshape(pairs, LANES, LANES)
    local_out = call(
        element_kernel,
        jax.ShapeDtypeStruct((pairs, chaos, LANES), f32),
        (fp, coupling, kl_lanes, stiff),
    )
    local_out = call(
        own_back_kernel,
        jax.ShapeDtypeStruct((pairs, chaos, LANES), f32),
        (own_pair, flux, int_weave, local_out),
        1,
        steps=steps,
        split=(1, 2),
    )
    result = call(
        functools.partial(die_back_kernel, part=part),
        jax.ShapeDtypeStruct(sent.shape, bf16),
        (die_pair, back_flux, die_weave, local_out),
        1,
        (
            pltpu.VMEM((pairs, chaos, LANES), f32),
            pltpu.VMEM((n_chaos, 256, nodes // 16), bf16),
        ),
        steps=steps,
        split=(1, 2),
    )
    returned = lax.all_to_all(result, "chaos", split_axis=0, concat_axis=0, tiled=True)
    return pl.pallas_call(
        receive_kernel,
        out_shape=jax.ShapeDtypeStruct((part, local_nodes), bf16),
        grid=(n_chaos,),
        in_specs=[pl.BlockSpec((1, 16 * part, nodes // 16), lambda c: (c, 0, 0))],
        out_specs=pl.BlockSpec((part, nodes), lambda c: (0, c)),
    )(returned)


def solution(mesh):
    in_specs = (
        P("chaos", "space"),
        P(("space", "chaos"), None),
        P(None, ("space", "chaos")),
        P(),
        P(),
        P(),
        P(),
        P(("space", "chaos")),
        P(("space", "chaos")),
        P(("space", "chaos")),
        P(("space", "chaos")),
        P(("space", "chaos"), None),
        P(("space", "chaos"), None),
        P(("space", "chaos"), None),
        P(("space", "chaos")),
        P(("space", "chaos")),
    )
    out_specs = P("chaos", "space")
    return jax.shard_map(local, mesh=mesh, in_specs=in_specs, out_specs=out_specs, check_vma=False)
```
